512 devices in a mesh: aux: 128 (over y, x_hi, z), pair: 4 (over x_lo, core).
Axes of the slice: x: 4 (x_hi: 2, x_lo: 2; x = x_hi * 2 + x_lo), y: 4, z: 16, core: 2. Of those that a mesh axis runs over, the one named last changes fastest.
Arguments:
- coeffs: bfloat16 [32768, 8192], P('aux', 'pair'), may hold values from -1 to 1
- occ_index: int32 [8192], P('pair'), may hold values from 0 to 1999
- vir_index: int32 [8192], P('pair'), may hold values from 0 to 19999
- eps_occ: float32 [2000], replicated, may hold values from -3 to -0.5
- eps_vir: float32 [20000], replicated, may hold values from 0.2 to 4
- frequencies: float32 [2], replicated, may hold values from 0.2 to 2
- offset: int32 [1], replicated, may hold values from 0 to 240
Outputs:
- polar: float32 [2048, 2, 32768], P('pair', None, 'aux')
The draws below stay inside these ranges and needn't reach their ends.
All inputs are finite; a program needn't handle non-finite values.
Results may differ from the reference program's by a relative error of at most 0.0026.
Values may be sent and summed in bfloat16 or wider, within the bound.
No kernel may reach another device: no remote copies, remote signals or barrier semaphores. Data moves between devices by JAX's collectives and lax.ppermute only.
A program may use at most 64 MiB of HBM per device.

```python
import math
import jax
import jax.numpy as jnp
from jax import lax

AUX_DEV = 256
ROWS_DEV = 16
NOCC = 2000
NVIR = 20000
NAUX = 32768
PAIRS = 8192
ROWS = 2048
N_AUX = 128


def set_ends(values, stream_key, smallest, top_value):
    longest = values.shape.index(max(values.shape))
    spots = []
    for shift in (0, 1):
        where = [jax.random.randint(jax.random.fold_in(stream_key, axis), (), 0, length) for axis, length in enumerate(values.shape)]
        where[longest] = (where[longest] + shift) % values.shape[longest]
        spots.append(tuple(where))
    return values.at[spots[0]].set(smallest).at[spots[1]].set(top_value)


def level_of(key, shape, pieces, least, largest):
    def one(dim, shards_of):
        heights = jax.random.uniform(jax.random.fold_in(jax.random.fold_in(key, 6), dim), (shards_of,), jnp.float32, least / len(pieces), largest / len(pieces))
        return jnp.repeat(jnp.exp(heights), shape[dim] // shards_of).reshape((-1,) + (1,) * (len(shape) - dim - 1))

    loudness = one(*pieces[0])
    for cut in pieces[1:]:
        loudness = loudness * one(*cut)
    return loudness


def centred(key, extent, width, bound, cuts=(), kind=jnp.bfloat16):
    drawn = jax.random.normal(key, extent, jnp.float32) * width
    if len(cuts) > 0:
        drawn = level_of(key, extent, cuts, -0.22, 0.18) * drawn
    return jnp.clip(drawn, min=-bound, max=bound).astype(kind)


def setup_inputs(seed: int = 0) -> dict:
    keys = jax.random.split(jax.random.key(seed), 8)
    return {
        "coeffs": centred(keys[0], (NAUX, PAIRS), 0.125, 1.0, ((0, 128), (1, 4))),
        "occ_index": set_ends(jax.random.randint(keys[1], (PAIRS,), 0, NOCC), jax.random.fold_in(keys[1], 1), 0, NOCC - 1).astype(jnp.int32),
        "vir_index": set_ends(jax.random.randint(keys[2], (PAIRS,), 0, NVIR), jax.random.fold_in(keys[2], 1), 0, NVIR - 1).astype(jnp.int32),
        "eps_occ": jnp.clip(jax.random.uniform(keys[3], (NOCC,), jnp.float32, -3.0, -0.5), -3.0, -0.5),
        "eps_vir": jnp.clip(jax.random.uniform(keys[4], (NVIR,), jnp.float32, 0.2, 4.0), 0.2, 4.0),
        "frequencies": jnp.clip(jnp.exp(jax.random.uniform(keys[5], (2,), jnp.float32, math.log(0.2), math.log(2.0))), 0.2, 2.0),
        "offset": jax.random.randint(keys[6], (1,), 0, AUX_DEV - ROWS_DEV + 1).astype(jnp.int32),
    }


def reference(coeffs, occ_index, vir_index, eps_occ, eps_vir, frequencies, offset):
    energy_gap = jnp.take(eps_vir, vir_index) - jnp.take(eps_occ, occ_index)
    rowid = jnp.arange(ROWS, dtype=jnp.int32)
    source = (rowid % N_AUX) * AUX_DEV + offset[0].astype(jnp.int32) + rowid // N_AUX
    slab = jnp.take(coeffs, source.astype(jnp.int32), axis=0)
    results = []
    for which in range(2):
        response = 2.0 * energy_gap / (energy_gap * energy_gap + frequencies[which] * frequencies[which])
        scaled = (coeffs.astype(jnp.float32) * response[None, :]).astype(jnp.bfloat16)
        product = lax.dot_general(slab, scaled, (((1,), (1,)), ((), ())), preferred_element_type=jnp.float32)
        results.append(product)
    return jnp.stack(results, axis=1)
```

```python
import functools

import jax
import jax.numpy as jnp
from jax import lax
from jax.experimental import pallas as pl
from jax.experimental.pallas import tpu as pltpu
from jax.sharding import Mesh
from jax.sharding import PartitionSpec as P

ROWS_DEV = 16
LANES = 128


def lookup(table, index):
    rows = -(-table.shape[0] // LANES)
    rows += -rows % 8
    grid = jnp.pad(table, (0, rows * LANES - table.shape[0])).reshape(rows, LANES)
    high = (index // LANES)[:, None] == jnp.arange(rows, dtype=jnp.int32)[None, :]
    low = (index % LANES)[:, None] == jnp.arange(LANES, dtype=jnp.int32)[None, :]
    picked = lax.dot_general(
        high.astype(jnp.float32),
        grid,
        (((1,), (0,)), ((), ())),
        precision=lax.Precision.HIGHEST,
        preferred_element_type=jnp.float32,
    )
    return jnp.sum(jnp.where(low, picked, 0.0), axis=1)


def product_kernel(own_ref, partner_ref, scaled_ref, out_ref):
    scaled = scaled_ref[0]
    depth = scaled.shape[-1]
    for side, ref in enumerate((own_ref, partner_ref)):
        rows = ref[...].reshape(-1, depth)
        product = lax.dot_general(
            rows, scaled, (((1,), (1,)), ((), ())), preferred_element_type=jnp.float32
        )
        product = product.reshape(ref.shape[0], 2, ref.shape[1] // 2, product.shape[-1])
        out_ref[0, 0, side] = product[:, 0]
        out_ref[0, 1, side] = product[:, 1]


def products(own, partner, scaled):
    n_z, n_rows, depth = own.shape
    n_y, columns, _ = scaled.shape
    block = (1, 2, 2, n_z, n_rows // 2, columns)
    whole = pl.BlockSpec((n_z, n_rows, depth), lambda y: (0, 0, 0))
    return pl.pallas_call(
        product_kernel,
        grid=(n_y,),
        in_specs=[whole, whole, pl.BlockSpec((1, columns, depth), lambda y: (y, 0, 0))],
        out_specs=pl.BlockSpec(block, lambda y: (y, 0, 0, 0, 0, 0)),
        out_shape=jax.ShapeDtypeStruct((n_y,) + block[1:], jnp.float32),
        compiler_params=pltpu.CompilerParams(vmem_limit_bytes=40 * 1024 * 1024),
        cost_estimate=pl.CostEstimate(
            flops=4 * n_z * n_rows * depth * columns * n_y,
            bytes_accessed=2 * columns * n_y * depth,
            transcendentals=0,
        ),
    )(own, partner, scaled)


def on_device(n_y, n_z, coeffs, occ_index, vir_index, eps_occ, eps_vir, frequencies, offset):
    aux_local, depth = coeffs.shape
    core = lax.axis_index("core")
    x_hi = lax.axis_index("x_hi")

    coeffs_y = lax.all_gather(coeffs, "y", axis=0)

    local_rows = lax.dynamic_slice_in_dim(coeffs, offset[0], ROWS_DEV, 0)
    local_rows = local_rows.reshape(2, 2, ROWS_DEV // 4, depth)
    first, second = local_rows[:, 0], local_rows[:, 1]
    parts = [jnp.where(core == 0, second, first), jnp.where(core == 0, first, second)]

    own = []
    for part in parts:
        part = part.reshape(1, ROWS_DEV // 2, depth)
        part = jnp.broadcast_to(part, (n_z,) + part.shape[1:])
        own.append(lax.all_to_all(part, "z", 0, 0, tiled=True))
    partner = [lax.ppermute(part, "x_hi", [(0, 1), (1, 0)]) for part in own]

    occ_index, vir_index, _ = lax.optimization_barrier((occ_index, vir_index, own[1]))
    energy_gap = lookup(eps_vir, vir_index) - lookup(eps_occ, occ_index)
    squares = frequencies * frequencies
    response = (
        2.0 * energy_gap[None, :] / (energy_gap[None, :] * energy_gap[None, :] + squares[:, None])
    )
    scaled = (coeffs_y[:, None].astype(jnp.float32) * response[None, :, None, :]).astype(
        jnp.bfloat16
    )
    scaled = scaled.reshape(n_y, 2 * aux_local, depth)

    away = products(own[0], partner[0], scaled)
    arrived = lax.ppermute(away, "core", [(0, 1), (1, 0)])
    kept = products(own[1], partner[1], scaled)
    total = (kept + arrived).reshape(n_y * 2, 2 * n_z * ROWS_DEV // 4, 2 * aux_local)
    total = lax.all_to_all(total, ("y", "x_lo"), 0, 0, tiled=True)
    total = total.reshape(n_y, 2, 2, n_z, ROWS_DEV // 4, 2, aux_local)
    total = total[:, 0] + total[:, 1]
    total = jnp.where(x_hi == 0, total, total[:, ::-1])
    polar = jnp.transpose(total, (3, 0, 1, 2, 4, 5))
    return polar.reshape(-1, 2, aux_local)


def solution(mesh):
    n_y = 4
    n_z = mesh.shape["aux"] // (2 * n_y)
    split = Mesh(
        mesh.devices.reshape(n_y, 2, n_z, 2, 2), ("y", "x_hi", "z", "x_lo", "core")
    )
    aux, pair = ("y", "x_hi", "z"), ("x_lo", "core")
    return jax.shard_map(
        functools.partial(on_device, n_y, n_z),
        mesh=split,
        in_specs=(P(aux, pair), P(pair), P(pair), P(), P(), P(), P()),
        out_specs=P(pair, None, aux),
        check_vma=False,
    )
```

```python
import functools

import jax
import jax.numpy as jnp
from jax import lax
from jax.experimental import pallas as pl
from jax.experimental.pallas import tpu as pltpu
from jax.sharding import Mesh
from jax.sharding import PartitionSpec as P

ROWS_DEV = 16
LANES = 128
VMEM = 24 * 1024 * 1024


def lookup(table, index):
    rows = -(-table.shape[0] // LANES)
    rows += -rows % 8
    grid = jnp.pad(table, (0, rows * LANES - table.shape[0])).reshape(rows, LANES)
    high = (index // LANES)[:, None] == jnp.arange(rows, dtype=jnp.int32)[None, :]
    low = (index % LANES)[:, None] == jnp.arange(LANES, dtype=jnp.int32)[None, :]
    picked = lax.dot_general(
        high.astype(jnp.float32),
        grid,
        (((1,), (0,)), ((), ())),
        precision=lax.Precision.HIGHEST,
        preferred_element_type=jnp.float32,
    )
    return jnp.sum(jnp.where(low, picked, 0.0), axis=1)


def scale_kernel(coeffs_ref, response_ref, out_ref):
    coeffs = coeffs_ref[0].astype(jnp.float32)
    aux_local = coeffs.shape[0]
    for w in range(2):
        out_ref[0, w * aux_local : (w + 1) * aux_local] = (
            coeffs * response_ref[w : w + 1, :]
        ).astype(jnp.bfloat16)


def scale(coeffs, response):
    n_y, aux_local, depth = coeffs.shape
    return pl.pallas_call(
        scale_kernel,
        grid=(n_y,),
        in_specs=[
            pl.BlockSpec((1, aux_local, depth), lambda y: (y, 0, 0)),
            pl.BlockSpec(response.shape, lambda y: (0, 0)),
        ],
        out_specs=pl.BlockSpec((1, 2 * aux_local, depth), lambda y: (y, 0, 0)),
        out_shape=jax.ShapeDtypeStruct((n_y, 2 * aux_local, depth), jnp.bfloat16),
        compiler_params=pltpu.CompilerParams(vmem_limit_bytes=VMEM),
        cost_estimate=pl.CostEstimate(
            flops=2 * aux_local * n_y * depth,
            bytes_accessed=6 * aux_local * n_y * depth,
            transcendentals=0,
        ),
    )(coeffs, response)


def product_kernel(rows_ref, scaled_ref, away_ref, kept_ref):
    product = lax.dot_general(
        rows_ref[...],
        scaled_ref[0],
        (((1,), (1,)), ((), ())),
        preferred_element_type=jnp.float32,
    )
    half = product.shape[0] // 2
    away_ref[0] = product[:half]
    kept_ref[0] = product[half:]


def products(rows, scaled):
    n_rows, depth = rows.shape
    n_y, columns, _ = scaled.shape
    out = (n_y, n_rows // 2, columns)
    return pl.pallas_call(
        product_kernel,
        grid=(n_y,),
        in_specs=[
            pl.BlockSpec((n_rows, depth), lambda y: (0, 0)),
            pl.BlockSpec((1, columns, depth), lambda y: (y, 0, 0)),
        ],
        out_specs=[pl.BlockSpec((1,) + out[1:], lambda y: (y, 0, 0))] * 2,
        out_shape=[jax.ShapeDtypeStruct(out, jnp.float32)] * 2,
        compiler_params=pltpu.CompilerParams(vmem_limit_bytes=VMEM),
        cost_estimate=pl.CostEstimate(
            flops=2 * n_rows * depth * columns * n_y,
            bytes_accessed=2 * columns * n_y * depth,
            transcendentals=0,
        ),
    )(rows, scaled)


def total_kernel(x_hi_ref, own_ref, partner_ref, out_ref):
    own, partner = [ref[:, 0, 0] + ref[:, 1, 0] for ref in (own_ref, partner_ref)]
    swap = x_hi_ref[0] == 1
    sides = jnp.where(swap, partner, own), jnp.where(swap, own, partner)
    n_y, n_z, _ = own.shape
    for y in range(n_y):
        for side in range(2):
            base = (2 * y + side) * n_z * 4
            for w in range(2):
                for half in range(2):
                    at = (2 * w + half) * LANES
                    out_ref[pl.ds(base + 2 * half + w, n_z, stride=4), :] = sides[side][
                        y, :, at : at + LANES
                    ]


def total_over_x(x_hi, own, partner):
    n_y, n_x, n_i, n_z, columns = own.shape
    block = pl.BlockSpec((n_y, n_x, 1, n_z, columns), lambda i, x: (0, 0, i, 0, 0))
    n_rows = n_y * 2 * n_z
    out = pl.pallas_call(
        total_kernel,
        grid_spec=pltpu.PrefetchScalarGridSpec(
            num_scalar_prefetch=1,
            grid=(n_i,),
            in_specs=[block, block],
            out_specs=pl.BlockSpec((n_rows * 4, LANES), lambda i, x: (i, 0)),
        ),
        out_shape=jax.ShapeDtypeStruct((n_i * n_rows * 4, LANES), jnp.float32),
        compiler_params=pltpu.CompilerParams(vmem_limit_bytes=VMEM),
    )(x_hi, own, partner)
    out = out.reshape(n_i * n_rows, 2, 2, LANES)
    return jnp.transpose(out, (0, 2, 1, 3)).reshape(-1, 2, 2 * LANES)


def on_device(n_y, n_z, coeffs, occ_index, vir_index, eps_occ, eps_vir, frequencies, offset):
    aux_local, depth = coeffs.shape
    core = lax.axis_index("core")
    x_hi = lax.axis_index("x_hi").reshape(1).astype(jnp.int32)
    swap = [(0, 1), (1, 0)]

    coeffs_y = lax.all_gather(coeffs, "y", axis=0)

    rows = lax.dynamic_slice_in_dim(coeffs, offset[0], ROWS_DEV, 0)
    rows = rows.reshape(2, 2, ROWS_DEV // 4, depth)
    first, second = rows[:, 0], rows[:, 1]
    rows = jnp.where(core == 0, jnp.stack([second, first]), jnp.stack([first, second]))
    rows = rows.reshape(ROWS_DEV, depth)

    last = jnp.broadcast_to(rows[-1].reshape(1, 2, -1), (n_z, 2, depth // 2))
    last = lax.all_to_all(last, "z", 0, 0, tiled=True)
    gathered = lax.all_gather(rows[:-1], "z", axis=0)
    gathered, last = lax.optimization_barrier((gathered, last))
    own = jnp.concatenate(
        [jnp.transpose(gathered, (1, 0, 2)), last.reshape(1, n_z, depth)], axis=0
    ).reshape(-1, depth)
    partner = lax.ppermute(own, "x_hi", swap)

    occ_index, vir_index, _ = lax.optimization_barrier((occ_index, vir_index, gathered))
    energy_gap = lookup(eps_vir, vir_index) - lookup(eps_occ, occ_index)
    squares = frequencies * frequencies
    response = (
        2.0 * energy_gap[None, :] / (energy_gap[None, :] * energy_gap[None, :] + squares[:, None])
    )
    scaled = scale(coeffs_y, response)

    totals = []
    for side in (own, partner):
        away, kept = products(side, scaled)
        total = (kept + lax.ppermute(away, "core", swap)).reshape(n_y * 2, -1, 2 * aux_local)
        total = lax.all_to_all(total, ("y", "x_lo"), 0, 0, tiled=True)
        totals.append(total.reshape(n_y, 2, ROWS_DEV // 4, n_z, 2 * aux_local))
    return total_over_x(x_hi, *totals)


def solution(mesh):
    n_y = 4
    n_z = mesh.shape["aux"] // (2 * n_y)
    split = Mesh(
        mesh.devices.reshape(n_y, 2, n_z, 2, 2), ("y", "x_hi", "z", "x_lo", "core")
    )
    aux, pair = ("y", "x_hi", "z"), ("x_lo", "core")
    return jax.shard_map(
        functools.partial(on_device, n_y, n_z),
        mesh=split,
        in_specs=(P(aux, pair), P(pair), P(pair), P(), P(), P(), P()),
        out_specs=P(pair, None, aux),
        check_vma=False,
    )
```

```python
import functools

import jax
import jax.numpy as jnp
from jax import lax
from jax.experimental import pallas as pl
from jax.experimental.pallas import tpu as pltpu
from jax.sharding import Mesh
from jax.sharding import PartitionSpec as P

ROWS_DEV = 16
LANES = 128
VMEM = 24 * 1024 * 1024
SMALL = pl.CostEstimate(flops=1, bytes_accessed=1, transcendentals=0)


def lookup(table, index):
    rows = -(-table.shape[0] // LANES)
    rows += -rows % 8
    grid = jnp.pad(table, (0, rows * LANES - table.shape[0])).reshape(rows, LANES)
    high = (index // LANES)[:, None] == jnp.arange(rows, dtype=jnp.int32)[None, :]
    low = (index % LANES)[:, None] == jnp.arange(LANES, dtype=jnp.int32)[None, :]
    picked = lax.dot_general(
        high.astype(jnp.float32),
        grid,
        (((1,), (0,)), ((), ())),
        precision=lax.Precision.HIGHEST,
        preferred_element_type=jnp.float32,
    )
    return jnp.sum(jnp.where(low, picked, 0.0), axis=1)


def scale_kernel(y_ref, *refs):
    del y_ref
    *coeffs_refs, response_ref, out_ref = refs
    for step, coeffs_ref in enumerate(coeffs_refs):

        @pl.when(pl.program_id(0) == step)
        def _(coeffs_ref=coeffs_ref):
            coeffs = coeffs_ref[...].astype(jnp.float32)
            aux_local = coeffs.shape[0]
            for w in range(2):
                out_ref[0, w * aux_local : (w + 1) * aux_local] = (
                    coeffs * response_ref[w : w + 1, :]
                ).astype(jnp.bfloat16)


def scale(y, coeffs, response):
    n_y = len(coeffs)
    aux_local, depth = coeffs[0].shape
    return pl.pallas_call(
        scale_kernel,
        grid_spec=pltpu.PrefetchScalarGridSpec(
            num_scalar_prefetch=1,
            grid=(n_y,),
            in_specs=[
                *[pl.BlockSpec((aux_local, depth), lambda i, y: (0, 0))] * n_y,
                pl.BlockSpec(response.shape, lambda i, y: (0, 0)),
            ],
            out_specs=pl.BlockSpec(
                (1, 2 * aux_local, depth), lambda i, y: (lax.rem(i + y[0], n_y), 0, 0)
            ),
        ),
        out_shape=jax.ShapeDtypeStruct((n_y, 2 * aux_local, depth), jnp.bfloat16),
        compiler_params=pltpu.CompilerParams(vmem_limit_bytes=VMEM),
        cost_estimate=SMALL,
    )(y, *coeffs, response)


def product_kernel(n_away, *refs):
    *rows_refs, scaled_ref, away_ref, kept_ref = refs
    depth = scaled_ref.shape[-1]
    rows = [ref[...].reshape(-1, depth) for ref in rows_refs]
    product = lax.dot_general(
        rows[0] if len(rows) == 1 else jnp.concatenate(rows, axis=0),
        scaled_ref[0],
        (((1,), (1,)), ((), ())),
        preferred_element_type=jnp.float32,
    )
    away_ref[0] = product[:n_away]
    kept_ref[0] = product[n_away:]


def products(rows, scaled, n_away):
    n_y, columns, depth = scaled.shape
    n_kept = sum(part.shape[0] for part in rows) - n_away
    return pl.pallas_call(
        functools.partial(product_kernel, n_away),
        grid=(n_y,),
        in_specs=[
            *[pl.BlockSpec(part.shape, lambda y: (0, 0)) for part in rows],
            pl.BlockSpec((1, columns, depth), lambda y: (y, 0, 0)),
        ],
        out_specs=[pl.BlockSpec((1, n, columns), lambda y: (y, 0, 0)) for n in (n_away, n_kept)],
        out_shape=[jax.ShapeDtypeStruct((n_y, n, columns), jnp.float32) for n in (n_away, n_kept)],
        compiler_params=pltpu.CompilerParams(vmem_limit_bytes=VMEM),
        cost_estimate=SMALL,
    )(*rows, scaled)


def total_kernel(x_hi_ref, parts_ref, out_ref):
    parts = parts_ref[:, :, :, 0].astype(jnp.float32)
    total = parts[:, 0] + parts[:, 1]
    swap = x_hi_ref[0] == 1
    n_y, _, n_z, _ = total.shape
    for y in range(n_y):
        for side in range(2):
            rows = jnp.where(swap, total[y, 1 - side], total[y, side])
            base = (2 * y + side) * n_z * 4
            for w in range(2):
                for half in range(2):
                    at = (2 * w + half) * LANES
                    out_ref[pl.ds(base + 2 * half + w, n_z, stride=4), :] = rows[:, at : at + LANES]


def total_over_x(x_hi, parts):
    n_y, n_x, n_sides, n_i, n_z, columns = parts.shape
    n_rows = n_y * n_sides * n_z
    out = pl.pallas_call(
        total_kernel,
        grid_spec=pltpu.PrefetchScalarGridSpec(
            num_scalar_prefetch=1,
            grid=(n_i,),
            in_specs=[
                pl.BlockSpec(
                    (n_y, n_x, n_sides, 1, n_z, columns), lambda i, x: (0, 0, 0, i, 0, 0)
                )
            ],
            out_specs=pl.BlockSpec((n_rows * 4, LANES), lambda i, x: (i, 0)),
        ),
        out_shape=jax.ShapeDtypeStruct((n_i * n_rows * 4, LANES), jnp.float32),
        compiler_params=pltpu.CompilerParams(vmem_limit_bytes=VMEM),
    )(x_hi, parts)
    out = out.reshape(n_i * n_rows, 2, 2, LANES)
    return jnp.transpose(out, (0, 2, 1, 3)).reshape(-1, 2, 2 * LANES)


def on_device(n_y, n_z, coeffs, occ_index, vir_index, eps_occ, eps_vir, frequencies, offset):
    aux_local, depth = coeffs.shape
    core = lax.axis_index("core")
    x_hi = lax.axis_index("x_hi").reshape(1).astype(jnp.int32)
    y = lax.axis_index("y").reshape(1).astype(jnp.int32)
    swap = [(0, 1), (1, 0)]

    rows = lax.dynamic_slice_in_dim(coeffs, offset[0], ROWS_DEV, 0)
    rows = rows.reshape(2, 2, ROWS_DEV // 4, depth)
    first, second = rows[:, 0], rows[:, 1]
    rows = jnp.where(core == 0, jnp.stack([second, first]), jnp.stack([first, second]))
    rows = rows.reshape(ROWS_DEV, depth)

    shifts = [[(i, (i - shift) % n_y) for i in range(n_y)] for shift in range(n_y)]
    coeffs_y = [coeffs] + [lax.ppermute(coeffs, "y", shifts[shift]) for shift in range(1, n_y)]

    last = jnp.concatenate([rows[-1:], lax.ppermute(rows[-1:], "x_hi", swap)], axis=0)
    gathered = lax.all_gather(rows[:-1], "z", axis=0)
    last, gathered = lax.optimization_barrier((last, gathered))
    own = jnp.transpose(gathered, (1, 0, 2)).reshape(-1, depth)
    partner = lax.ppermute(own, "x_hi", swap)
    last = jnp.broadcast_to(last[None], (n_z, 2, depth))
    last = lax.all_to_all(last, "z", 0, 0, tiled=True)
    last = jnp.transpose(last, (1, 0, 2))

    occ_index, vir_index, _ = lax.optimization_barrier((occ_index, vir_index, gathered))
    energy_gap = lookup(eps_vir, vir_index) - lookup(eps_occ, occ_index)
    squares = frequencies * frequencies
    response = (
        2.0 * energy_gap[None, :] / (energy_gap[None, :] * energy_gap[None, :] + squares[:, None])
    )
    scaled = scale(y, coeffs_y, response)

    n_away = ROWS_DEV // 2 * n_z
    away, kept = products([own, last[0]], scaled, n_away)
    arrived = lax.ppermute(away, "core", swap)
    totals = [kept + arrived]
    away, kept = products([partner, last[1]], scaled, n_away)
    totals.append(kept + lax.ppermute(away, "core", swap))
    totals = jnp.stack([t.reshape(n_y * 2, -1, 2 * aux_local) for t in totals], axis=1)
    totals = lax.all_to_all(totals, ("y", "x_lo"), 0, 0, tiled=True)
    totals = totals.reshape(n_y, 2, 2, ROWS_DEV // 4, n_z, 2 * aux_local)
    return total_over_x(x_hi, totals)


def solution(mesh):
    n_y = 4
    n_z = mesh.shape["aux"] // (2 * n_y)
    split = Mesh(
        mesh.devices.reshape(n_y, 2, n_z, 2, 2), ("y", "x_hi", "z", "x_lo", "core")
    )
    aux, pair = ("y", "x_hi", "z"), ("x_lo", "core")
    return jax.shard_map(
        functools.partial(on_device, n_y, n_z),
        mesh=split,
        in_specs=(P(aux, pair), P(pair), P(pair), P(), P(), P(), P()),
        out_specs=P(pair, None, aux),
        check_vma=False,
    )
```

```python
import functools

import jax
import jax.numpy as jnp
from jax import lax
from jax.experimental import pallas as pl
from jax.experimental.pallas import tpu as pltpu
from jax.sharding import Mesh
from jax.sharding import PartitionSpec as P

ROWS_DEV = 16
LANES = 128
SENT = jnp.bfloat16
VMEM = 24 * 1024 * 1024
SMALL = pl.CostEstimate(flops=1, bytes_accessed=1, transcendentals=0)


def lookup(table, index):
    rows = -(-table.shape[0] // LANES)
    rows += -rows % 8
    grid = jnp.pad(table, (0, rows * LANES - table.shape[0])).reshape(rows, LANES)
    high = (index // LANES)[:, None] == jnp.arange(rows, dtype=jnp.int32)[None, :]
    low = (index % LANES)[:, None] == jnp.arange(LANES, dtype=jnp.int32)[None, :]
    picked = lax.dot_general(
        high.astype(jnp.float32),
        grid,
        (((1,), (0,)), ((), ())),
        precision=lax.Precision.HIGHEST,
        preferred_element_type=jnp.float32,
    )
    return jnp.sum(jnp.where(low, picked, 0.0), axis=1)


def scale_kernel(y_ref, *refs):
    del y_ref
    *coeffs_refs, response_ref, out_ref = refs
    for step, coeffs_ref in enumerate(coeffs_refs):

        @pl.when(pl.program_id(0) == step)
        def _(coeffs_ref=coeffs_ref):
            coeffs = coeffs_ref[...].astype(jnp.float32)
            aux_local = coeffs.shape[0]
            for w in range(2):
                out_ref[0, w * aux_local : (w + 1) * aux_local] = (
                    coeffs * response_ref[w : w + 1, :]
                ).astype(jnp.bfloat16)


def scale(y, coeffs, response):
    n_y = len(coeffs)
    aux_local, depth = coeffs[0].shape
    return pl.pallas_call(
        scale_kernel,
        grid_spec=pltpu.PrefetchScalarGridSpec(
            num_scalar_prefetch=1,
            grid=(n_y,),
            in_specs=[
                *[pl.BlockSpec((aux_local, depth), lambda i, y: (0, 0))] * n_y,
                pl.BlockSpec(response.shape, lambda i, y: (0, 0)),
            ],
            out_specs=pl.BlockSpec(
                (1, 2 * aux_local, depth), lambda i, y: (lax.rem(i + y[0], n_y), 0, 0)
            ),
        ),
        out_shape=jax.ShapeDtypeStruct((n_y, 2 * aux_local, depth), jnp.bfloat16),
        compiler_params=pltpu.CompilerParams(vmem_limit_bytes=VMEM),
        cost_estimate=SMALL,
    )(y, *coeffs, response)


def product_kernel(near_ref, far_ref, scaled_ref, away_ref, kept_ref):
    size = near_ref.shape[0] // 4
    rows = [ref[at * size : (at + 1) * size] for at in range(4) for ref in (near_ref, far_ref)]
    product = lax.dot_general(
        jnp.concatenate(rows, axis=0),
        scaled_ref[0],
        (((1,), (1,)), ((), ())),
        preferred_element_type=jnp.float32,
    )
    half = product.shape[0] // 2
    away_ref[0] = product[:half]
    kept_ref[0] = product[half:]


def products(near, far, scaled):
    n_rows, depth = near.shape
    n_y, columns, _ = scaled.shape
    rows = pl.BlockSpec((n_rows, depth), lambda y: (0, 0))
    return pl.pallas_call(
        product_kernel,
        grid=(n_y,),
        in_specs=[rows, rows, pl.BlockSpec((1, columns, depth), lambda y: (y, 0, 0))],
        out_specs=[pl.BlockSpec((1, n_rows, columns), lambda y: (y, 0, 0))] * 2,
        out_shape=[jax.ShapeDtypeStruct((n_y, n_rows, columns), jnp.float32)] * 2,
        compiler_params=pltpu.CompilerParams(vmem_limit_bytes=VMEM),
        cost_estimate=SMALL,
    )(near, far, scaled)


def add_kernel(*refs):
    *refs, out_ref = refs
    for side in range(2):
        total = refs[2 * side][0] + refs[2 * side + 1][0]
        total = total.reshape((2, -1) + total.shape[1:])
        out_ref[:, side] = total.astype(out_ref.dtype)


def add_cores(own, partner):
    n_y, n_rows, columns = own[0].shape
    return pl.pallas_call(
        add_kernel,
        grid=(n_y,),
        in_specs=[pl.BlockSpec((1, n_rows, columns), lambda y: (y, 0, 0))] * 4,
        out_specs=pl.BlockSpec((2, 2, n_rows // 2, columns), lambda y: (y, 0, 0, 0)),
        out_shape=jax.ShapeDtypeStruct((2 * n_y, 2, n_rows // 2, columns), SENT),
        compiler_params=pltpu.CompilerParams(vmem_limit_bytes=VMEM),
        cost_estimate=SMALL,
    )(*own, *partner)


def total_kernel(place_ref, parts_ref, out_ref):
    n_y, _, _, _, _, n_z, _ = parts_ref.shape
    x_hi, parity = place_ref[0], place_ref[1]
    for y in range(n_y):
        for side in range(2):
            for odd in range(2):
                at = jnp.bitwise_xor(side, x_hi), jnp.bitwise_xor(odd, parity)
                rows = [parts_ref[y, x, at[0], at[1], 0].astype(jnp.float32) for x in range(2)]
                rows = rows[0] + rows[1]
                base = ((2 * y + side) * 2 * n_z + odd) * 4
                for w in range(2):
                    for half in range(2):
                        c = (2 * w + half) * LANES
                        out_ref[pl.ds(base + 2 * half + w, n_z, stride=8), :] = rows[
                            :, c : c + LANES
                        ]


def total_over_x(place, parts):
    n_y, n_x, n_sides, n_parities, n_i, n_z, columns = parts.shape
    n_rows = n_y * n_sides * n_parities * n_z
    out = pl.pallas_call(
        total_kernel,
        grid_spec=pltpu.PrefetchScalarGridSpec(
            num_scalar_prefetch=1,
            grid=(n_i,),
            in_specs=[
                pl.BlockSpec(
                    (n_y, n_x, n_sides, n_parities, 1, n_z, columns),
                    lambda i, place: (0, 0, 0, 0, i, 0, 0),
                )
            ],
            out_specs=pl.BlockSpec((n_rows * 4, LANES), lambda i, place: (i, 0)),
        ),
        out_shape=jax.ShapeDtypeStruct((n_i * n_rows * 4, LANES), jnp.float32),
        compiler_params=pltpu.CompilerParams(vmem_limit_bytes=VMEM),
    )(place, parts)
    out = out.reshape(n_i * n_rows, 2, 2, LANES)
    return jnp.transpose(out, (0, 2, 1, 3)).reshape(-1, 2, 2 * LANES)


def on_device(n_y, n_z, coeffs, occ_index, vir_index, eps_occ, eps_vir, frequencies, offset):
    aux_local, depth = coeffs.shape
    core = lax.axis_index("core")
    place = jnp.stack([lax.axis_index("x_hi"), lax.axis_index("parity")]).astype(jnp.int32)
    y = lax.axis_index("y").reshape(1).astype(jnp.int32)
    swap = [(0, 1), (1, 0)]

    rows = lax.dynamic_slice_in_dim(coeffs, offset[0], ROWS_DEV, 0)
    rows = rows.reshape(2, 2, ROWS_DEV // 4, depth)
    first, second = rows[:, 0], rows[:, 1]
    rows = jnp.where(core == 0, jnp.stack([second, first]), jnp.stack([first, second]))
    rows = rows.reshape(ROWS_DEV, depth)

    shifts = [[(i, (i - shift) % n_y) for i in range(n_y)] for shift in range(n_y)]
    coeffs_y = [coeffs] + [lax.ppermute(coeffs, "y", shifts[shift]) for shift in range(1, n_y)]

    z = ("half_z", "parity")
    gathered = lax.all_gather(rows, "half_z", axis=0)
    near = jnp.transpose(gathered, (1, 0, 2)).reshape(-1, depth)
    middle = near.shape[0] // 2
    near_partner = lax.ppermute(near, "x_hi", swap)
    far = jnp.concatenate(
        [
            lax.ppermute(near[:middle], z, [(i, (i + 1) % n_z) for i in range(n_z)]),
            lax.ppermute(near[middle:], z, [(i, (i - 1) % n_z) for i in range(n_z)]),
        ],
        axis=0,
    )
    far_partner = lax.ppermute(far, "x_hi", swap)

    occ_index, vir_index, _ = lax.optimization_barrier((occ_index, vir_index, gathered))
    energy_gap = lookup(eps_vir, vir_index) - lookup(eps_occ, occ_index)
    squares = frequencies * frequencies
    response = (
        2.0 * energy_gap[None, :] / (energy_gap[None, :] * energy_gap[None, :] + squares[:, None])
    )
    scaled = scale(y, coeffs_y, response)

    sides = []
    for side in ((near, far), (near_partner, far_partner)):
        away, kept = products(*side, scaled)
        sides.append((kept, lax.ppermute(away, "core", swap)))
    parts = lax.all_to_all(add_cores(*sides), ("y", "x_lo"), 0, 0, tiled=True)
    parts = parts.reshape(n_y, 2, 2, 2, ROWS_DEV // 4, n_z // 2, 2 * aux_local)
    return total_over_x(place, parts)


def solution(mesh):
    n_y = 4
    n_z = mesh.shape["aux"] // (2 * n_y)
    split = Mesh(
        mesh.devices.reshape(n_y, 2, n_z // 2, 2, 2, 2),
        ("y", "x_hi", "half_z", "parity", "x_lo", "core"),
    )
    aux, pair = ("y", "x_hi", "half_z", "parity"), ("x_lo", "core")
    return jax.shard_map(
        functools.partial(on_device, n_y, n_z),
        mesh=split,
        in_specs=(P(aux, pair), P(pair), P(pair), P(), P(), P(), P()),
        out_specs=P(pair, None, aux),
        check_vma=False,
    )
```

```python
import functools

import jax
import jax.numpy as jnp
from jax import lax
from jax.experimental import pallas as pl
from jax.experimental.pallas import tpu as pltpu
from jax.sharding import Mesh
from jax.sharding import PartitionSpec as P

ROWS_DEV = 16
LANES = 128
SENT = jnp.bfloat16
VMEM = 16 * 1024 * 1024
SMALL = pl.CostEstimate(flops=1, bytes_accessed=1, transcendentals=0)


def lookup(table, index):
    rows = -(-table.shape[0] // LANES)
    rows += -rows % 8
    grid = jnp.pad(table, (0, rows * LANES - table.shape[0])).reshape(rows, LANES)
    high = (index // LANES)[:, None] == jnp.arange(rows, dtype=jnp.int32)[None, :]
    low = (index % LANES)[:, None] == jnp.arange(LANES, dtype=jnp.int32)[None, :]
    picked = lax.dot_general(
        high.astype(jnp.float32),
        grid,
        (((1,), (0,)), ((), ())),
        precision=lax.Precision.HIGHEST,
        preferred_element_type=jnp.float32,
    )
    return jnp.sum(jnp.where(low, picked, 0.0), axis=1)


def scale_kernel(coeffs_ref, response_ref, out_ref):
    coeffs = coeffs_ref[0].astype(jnp.float32)
    aux_local = coeffs.shape[0]
    for w in range(2):
        out_ref[0, w * aux_local : (w + 1) * aux_local] = (
            coeffs * response_ref[w : w + 1, :]
        ).astype(jnp.bfloat16)


def scale(coeffs, response):
    n_y, aux_local, depth = coeffs.shape
    return pl.pallas_call(
        scale_kernel,
        grid=(n_y,),
        in_specs=[
            pl.BlockSpec((1, aux_local, depth), lambda y: (y, 0, 0)),
            pl.BlockSpec(response.shape, lambda y: (0, 0)),
        ],
        out_specs=pl.BlockSpec((1, 2 * aux_local, depth), lambda y: (y, 0, 0)),
        out_shape=jax.ShapeDtypeStruct((n_y, 2 * aux_local, depth), jnp.bfloat16),
        compiler_params=pltpu.CompilerParams(vmem_limit_bytes=VMEM),
        cost_estimate=SMALL,
    )(coeffs, response)


def product_kernel(near_ref, far_ref, scaled_ref, away_ref, kept_ref):
    size = near_ref.shape[0] // 4
    rows = [ref[at * size : (at + 1) * size] for at in range(4) for ref in (near_ref, far_ref)]
    product = lax.dot_general(
        jnp.concatenate(rows, axis=0),
        scaled_ref[0],
        (((1,), (1,)), ((), ())),
        preferred_element_type=jnp.float32,
    )
    half = product.shape[0] // 2
    away_ref[0] = product[:half]
    kept_ref[0] = product[half:]


def products(near, far, scaled):
    n_rows, depth = near.shape
    n_y, columns, _ = scaled.shape
    rows = pl.BlockSpec((n_rows, depth), lambda y: (0, 0))
    return pl.pallas_call(
        product_kernel,
        grid=(n_y,),
        in_specs=[rows, rows, pl.BlockSpec((1, columns, depth), lambda y: (y, 0, 0))],
        out_specs=[pl.BlockSpec((1, n_rows, columns), lambda y: (y, 0, 0))] * 2,
        out_shape=[jax.ShapeDtypeStruct((n_y, n_rows, columns), jnp.float32)] * 2,
        compiler_params=pltpu.CompilerParams(vmem_limit_bytes=VMEM),
        cost_estimate=SMALL,
    )(near, far, scaled)


def add_kernel(*refs):
    *refs, out_ref = refs
    for side in range(2):
        total = refs[2 * side][0] + refs[2 * side + 1][0]
        total = total.reshape((2, -1) + total.shape[1:])
        out_ref[:, side] = total.astype(out_ref.dtype)


def add_cores(own, partner):
    n_y, n_rows, columns = own[0].shape
    return pl.pallas_call(
        add_kernel,
        grid=(n_y,),
        in_specs=[pl.BlockSpec((1, n_rows, columns), lambda y: (y, 0, 0))] * 4,
        out_specs=pl.BlockSpec((2, 2, n_rows // 2, columns), lambda y: (y, 0, 0, 0)),
        out_shape=jax.ShapeDtypeStruct((2 * n_y, 2, n_rows // 2, columns), SENT),
        compiler_params=pltpu.CompilerParams(vmem_limit_bytes=VMEM),
        cost_estimate=SMALL,
    )(*own, *partner)


def total_kernel(place_ref, parts_ref, out_ref):
    n_y, _, _, _, _, n_z, _ = parts_ref.shape
    x_hi, parity = place_ref[0], place_ref[1]
    for y in range(n_y):
        for side in range(2):
            for odd in range(2):
                at = jnp.bitwise_xor(side, x_hi), jnp.bitwise_xor(odd, parity)
                rows = [parts_ref[y, x, at[0], at[1], 0].astype(jnp.float32) for x in range(2)]
                rows = rows[0] + rows[1]
                base = ((2 * y + side) * 2 * n_z + odd) * 4
                for w in range(2):
                    for half in range(2):
                        c = (2 * w + half) * LANES
                        out_ref[pl.ds(base + 2 * half + w, n_z, stride=8), :] = rows[
                            :, c : c + LANES
                        ]


def total_over_x(place, parts):
    n_y, n_x, n_sides, n_parities, n_i, n_z, columns = parts.shape
    n_rows = n_y * n_sides * n_parities * n_z
    out = pl.pallas_call(
        total_kernel,
        grid_spec=pltpu.PrefetchScalarGridSpec(
            num_scalar_prefetch=1,
            grid=(n_i,),
            in_specs=[
                pl.BlockSpec(
                    (n_y, n_x, n_sides, n_parities, 1, n_z, columns),
                    lambda i, place: (0, 0, 0, 0, i, 0, 0),
                )
            ],
            out_specs=pl.BlockSpec((n_rows * 4, LANES), lambda i, place: (i, 0)),
        ),
        out_shape=jax.ShapeDtypeStruct((n_i * n_rows * 4, LANES), jnp.float32),
        compiler_params=pltpu.CompilerParams(vmem_limit_bytes=VMEM),
    )(place, parts)
    out = out.reshape(n_i * n_rows, 2, 2, LANES)
    return jnp.transpose(out, (0, 2, 1, 3)).reshape(-1, 2, 2 * LANES)


def on_device(n_y, n_z, coeffs, occ_index, vir_index, eps_occ, eps_vir, frequencies, offset):
    aux_local, depth = coeffs.shape
    core = lax.axis_index("core")
    place = jnp.stack([lax.axis_index("x_hi"), lax.axis_index("parity")]).astype(jnp.int32)
    swap = [(0, 1), (1, 0)]

    rows = lax.dynamic_slice_in_dim(coeffs, offset[0], ROWS_DEV, 0)
    rows = rows.reshape(2, 2, ROWS_DEV // 4, depth)
    first, second = rows[:, 0], rows[:, 1]
    rows = jnp.where(core == 0, jnp.stack([second, first]), jnp.stack([first, second]))
    rows = rows.reshape(ROWS_DEV, depth)

    coeffs_y = jnp.broadcast_to(coeffs[None], (n_y, aux_local, depth))
    coeffs_y = lax.all_to_all(coeffs_y, "y", 0, 0, tiled=True)

    gathered = lax.all_gather(rows, "half_z", axis=0)
    near = jnp.transpose(gathered, (1, 0, 2)).reshape(-1, depth)
    near_partner = lax.ppermute(near, "x_hi", swap)
    far = lax.ppermute(near, "parity", swap)
    far_partner = lax.ppermute(far, "x_hi", swap)

    energy_gap = lookup(eps_vir, vir_index) - lookup(eps_occ, occ_index)
    squares = frequencies * frequencies
    response = (
        2.0 * energy_gap[None, :] / (energy_gap[None, :] * energy_gap[None, :] + squares[:, None])
    )
    scaled = scale(coeffs_y, response)

    sides = []
    for side in ((near, far), (near_partner, far_partner)):
        away, kept = products(*side, scaled)
        sides.append((kept, lax.ppermute(away, "core", swap)))
    parts = lax.all_to_all(add_cores(*sides), ("y", "x_lo"), 0, 0, tiled=True)
    parts = parts.reshape(n_y, 2, 2, 2, ROWS_DEV // 4, n_z // 2, 2 * aux_local)
    return total_over_x(place, parts)


def solution(mesh):
    n_y = 4
    n_z = mesh.shape["aux"] // (2 * n_y)
    split = Mesh(
        mesh.devices.reshape(n_y, 2, n_z // 2, 2, 2, 2),
        ("y", "x_hi", "half_z", "parity", "x_lo", "core"),
    )
    aux, pair = ("y", "x_hi", "half_z", "parity"), ("x_lo", "core")
    return jax.shard_map(
        functools.partial(on_device, n_y, n_z),
        mesh=split,
        in_specs=(P(aux, pair), P(pair), P(pair), P(), P(), P(), P()),
        out_specs=P(pair, None, aux),
        check_vma=False,
    )
```

```python
import functools
import itertools

import jax
import jax.numpy as jnp
from jax import lax
from jax.experimental import pallas as pl
from jax.experimental.pallas import tpu as pltpu
from jax.sharding import Mesh
from jax.sharding import PartitionSpec as P

ROWS_DEV = 16
LANES = 128
SENT = jnp.bfloat16
VMEM = 16 * 1024 * 1024
SMALL = pl.CostEstimate(flops=1, bytes_accessed=1, transcendentals=0)


def lookup(table, index):
    rows = -(-table.shape[0] // LANES)
    rows += -rows % 8
    grid = jnp.pad(table, (0, rows * LANES - table.shape[0])).reshape(rows, LANES)
    high = (index // LANES)[:, None] == jnp.arange(rows, dtype=jnp.int32)[None, :]
    low = (index % LANES)[:, None] == jnp.arange(LANES, dtype=jnp.int32)[None, :]
    picked = lax.dot_general(
        high.astype(jnp.float32),
        grid,
        (((1,), (0,)), ((), ())),
        precision=lax.Precision.HIGHEST,
        preferred_element_type=jnp.float32,
    )
    return jnp.sum(jnp.where(low, picked, 0.0), axis=1)


def scale_kernel(coeffs_ref, response_ref, out_ref):
    coeffs = coeffs_ref[0].astype(jnp.float32)
    aux_local = coeffs.shape[0]
    for w in range(2):
        out_ref[0, w * aux_local : (w + 1) * aux_local] = (
            coeffs * response_ref[w : w + 1, :]
        ).astype(jnp.bfloat16)


def scale(coeffs, response):
    n_y, aux_local, depth = coeffs.shape
    return pl.pallas_call(
        scale_kernel,
        grid=(n_y,),
        in_specs=[
            pl.BlockSpec((1, aux_local, depth), lambda y: (y, 0, 0)),
            pl.BlockSpec(response.shape, lambda y: (0, 0)),
        ],
        out_specs=pl.BlockSpec((1, 2 * aux_local, depth), lambda y: (y, 0, 0)),
        out_shape=jax.ShapeDtypeStruct((n_y, 2 * aux_local, depth), jnp.bfloat16),
        compiler_params=pltpu.CompilerParams(vmem_limit_bytes=VMEM),
        cost_estimate=SMALL,
    )(coeffs, response)


def product_kernel(near_ref, far_ref, scaled_ref, away_ref, kept_ref):
    size = near_ref.shape[0] // 4
    rows = [ref[at * size : (at + 1) * size] for at in range(4) for ref in (near_ref, far_ref)]
    rows = jnp.concatenate(rows, axis=0)
    half = rows.shape[0] // 2
    for y in range(scaled_ref.shape[0]):
        product = lax.dot_general(
            rows, scaled_ref[y], (((1,), (1,)), ((), ())), preferred_element_type=jnp.float32
        )
        away_ref[y] = product[:half]
        kept_ref[y] = product[half:]


def products(near, far, scaled):
    n_rows, depth = near.shape
    n_y, columns, _ = scaled.shape
    rows = pl.BlockSpec((n_rows, depth), lambda y: (0, 0))
    return pl.pallas_call(
        product_kernel,
        grid=(n_y // 2,),
        in_specs=[rows, rows, pl.BlockSpec((2, columns, depth), lambda y: (y, 0, 0))],
        out_specs=[pl.BlockSpec((2, n_rows, columns), lambda y: (y, 0, 0))] * 2,
        out_shape=[jax.ShapeDtypeStruct((n_y, n_rows, columns), jnp.float32)] * 2,
        compiler_params=pltpu.CompilerParams(vmem_limit_bytes=VMEM),
        cost_estimate=SMALL,
    )(near, far, scaled)


def add_kernel(*refs):
    *refs, out_ref = refs
    for side in range(2):
        total = refs[2 * side][...] + refs[2 * side + 1][...]
        total = total.reshape((out_ref.shape[0], -1, total.shape[-1]))
        out_ref[:, side] = total.astype(out_ref.dtype)


def add_cores(own, partner):
    n_y, n_rows, columns = own[0].shape
    return pl.pallas_call(
        add_kernel,
        grid=(n_y // 2,),
        in_specs=[pl.BlockSpec((2, n_rows, columns), lambda y: (y, 0, 0))] * 4,
        out_specs=pl.BlockSpec((4, 2, n_rows // 2, columns), lambda y: (y, 0, 0, 0)),
        out_shape=jax.ShapeDtypeStruct((2 * n_y, 2, n_rows // 2, columns), SENT),
        compiler_params=pltpu.CompilerParams(vmem_limit_bytes=VMEM),
        cost_estimate=SMALL,
    )(*own, *partner)


def total_kernel(place_ref, parts_ref, out_ref):
    n_y, _, _, _, n_i, n_z, _ = parts_ref.shape
    x_hi, parity = place_ref[0], place_ref[1]
    for i, y, side, odd in itertools.product(range(n_i), range(n_y), range(2), range(2)):
        at = jnp.bitwise_xor(side, x_hi), jnp.bitwise_xor(odd, parity)
        rows = [parts_ref[y, x, at[0], at[1], i].astype(jnp.float32) for x in range(2)]
        rows = rows[0] + rows[1]
        base = (((n_y * i + y) * 2 + side) * 2 * n_z + odd) * 4
        for w in range(2):
            for half in range(2):
                c = (2 * w + half) * LANES
                out_ref[pl.ds(base + 2 * half + w, n_z, stride=8), :] = rows[:, c : c + LANES]


def total_over_x(place, parts):
    n_y, n_x, n_sides, n_parities, n_i, n_z, columns = parts.shape
    n_rows = n_y * n_sides * n_parities * n_z
    out = pl.pallas_call(
        total_kernel,
        grid_spec=pltpu.PrefetchScalarGridSpec(
            num_scalar_prefetch=1,
            grid=(n_i // 2,),
            in_specs=[
                pl.BlockSpec(
                    (n_y, n_x, n_sides, n_parities, 2, n_z, columns),
                    lambda i, place: (0, 0, 0, 0, i, 0, 0),
                )
            ],
            out_specs=pl.BlockSpec((2 * n_rows * 4, LANES), lambda i, place: (i, 0)),
        ),
        out_shape=jax.ShapeDtypeStruct((n_i * n_rows * 4, LANES), jnp.float32),
        compiler_params=pltpu.CompilerParams(vmem_limit_bytes=VMEM),
    )(place, parts)
    out = out.reshape(n_i * n_rows, 2, 2, LANES)
    return jnp.transpose(out, (0, 2, 1, 3)).reshape(-1, 2, 2 * LANES)


def on_device(n_y, n_z, coeffs, occ_index, vir_index, eps_occ, eps_vir, frequencies, offset):
    aux_local, depth = coeffs.shape
    core = lax.axis_index("core")
    place = jnp.stack([lax.axis_index("x_hi"), lax.axis_index("parity")]).astype(jnp.int32)
    swap = [(0, 1), (1, 0)]

    rows = lax.dynamic_slice_in_dim(coeffs, offset[0], ROWS_DEV, 0)
    rows = rows.reshape(2, 2, ROWS_DEV // 4, depth)
    first, second = rows[:, 0], rows[:, 1]
    rows = jnp.where(core == 0, jnp.stack([second, first]), jnp.stack([first, second]))
    rows = rows.reshape(ROWS_DEV, depth)

    coeffs_y = jnp.broadcast_to(coeffs[None], (n_y, aux_local, depth))
    coeffs_y = lax.all_to_all(coeffs_y, "y", 0, 0, tiled=True)

    gathered = lax.all_gather(rows, "half_z", axis=0)
    near = jnp.transpose(gathered, (1, 0, 2)).reshape(-1, depth)
    near_partner = lax.ppermute(near, "x_hi", swap)
    far = lax.ppermute(near, "parity", swap)
    far_partner = lax.ppermute(far, "x_hi", swap)

    energy_gap = lookup(eps_vir, vir_index) - lookup(eps_occ, occ_index)
    squares = frequencies * frequencies
    response = (
        2.0 * energy_gap[None, :] / (energy_gap[None, :] * energy_gap[None, :] + squares[:, None])
    )
    scaled = scale(coeffs_y, response)

    sides = []
    for side in ((near, far), (near_partner, far_partner)):
        away, kept = products(*side, scaled)
        sides.append((kept, lax.ppermute(away, "core", swap)))
    parts = lax.all_to_all(add_cores(*sides), ("y", "x_lo"), 0, 0, tiled=True)
    parts = parts.reshape(n_y, 2, 2, 2, ROWS_DEV // 4, n_z // 2, 2 * aux_local)
    return total_over_x(place, parts)


def solution(mesh):
    n_y = 4
    n_z = mesh.shape["aux"] // (2 * n_y)
    split = Mesh(
        mesh.devices.reshape(n_y, 2, n_z // 2, 2, 2, 2),
        ("y", "x_hi", "half_z", "parity", "x_lo", "core"),
    )
    aux, pair = ("y", "x_hi", "half_z", "parity"), ("x_lo", "core")
    return jax.shard_map(
        functools.partial(on_device, n_y, n_z),
        mesh=split,
        in_specs=(P(aux, pair), P(pair), P(pair), P(), P(), P(), P()),
        out_specs=P(pair, None, aux),
        check_vma=False,
    )
```

```python
import functools
import itertools

import jax
import jax.numpy as jnp
from jax import lax
from jax.experimental import pallas as pl
from jax.experimental.pallas import tpu as pltpu
from jax.sharding import Mesh
from jax.sharding import PartitionSpec as P

ROWS_DEV = 16
LANES = 128
SENT = jnp.bfloat16
VMEM = 16 * 1024 * 1024
SMALL = pl.CostEstimate(flops=1, bytes_accessed=1, transcendentals=0)


def lookup(table, index):
    rows = -(-table.shape[0] // LANES)
    rows += -rows % 8
    grid = jnp.pad(table, (0, rows * LANES - table.shape[0])).reshape(rows, LANES)
    high = (index // LANES)[:, None] == jnp.arange(rows, dtype=jnp.int32)[None, :]
    low = (index % LANES)[:, None] == jnp.arange(LANES, dtype=jnp.int32)[None, :]
    picked = lax.dot_general(
        high.astype(jnp.float32),
        grid,
        (((1,), (0,)), ((), ())),
        precision=lax.Precision.HIGHEST,
        preferred_element_type=jnp.float32,
    )
    return jnp.sum(jnp.where(low, picked, 0.0), axis=1)


def repeat_kernel(source_ref, out_ref, block_ref, sems):
    fetch = pltpu.make_async_copy(source_ref, block_ref, sems.at[0])
    fetch.start()
    fetch.wait()
    copies = [
        pltpu.make_async_copy(block_ref, out_ref.at[at], sems.at[at])
        for at in range(out_ref.shape[0])
    ]
    for copy in copies:
        copy.start()
    for copy in copies:
        copy.wait()


def repeat(block, times):
    return pl.pallas_call(
        repeat_kernel,
        in_specs=[pl.BlockSpec(memory_space=pltpu.HBM)],
        out_specs=pl.BlockSpec(memory_space=pltpu.HBM),
        out_shape=jax.ShapeDtypeStruct((times,) + block.shape, block.dtype),
        scratch_shapes=[
            pltpu.VMEM(block.shape, block.dtype),
            pltpu.SemaphoreType.DMA((times,)),
        ],
        compiler_params=pltpu.CompilerParams(vmem_limit_bytes=60 * 1024 * 1024),
        cost_estimate=SMALL,
    )(block)


def scale_kernel(coeffs_ref, response_ref, out_ref):
    coeffs = coeffs_ref[0].astype(jnp.float32)
    aux_local = coeffs.shape[0]
    for w in range(2):
        out_ref[0, w * aux_local : (w + 1) * aux_local] = (
            coeffs * response_ref[w : w + 1, :]
        ).astype(jnp.bfloat16)


def scale(coeffs, response):
    n_y, aux_local, depth = coeffs.shape
    return pl.pallas_call(
        scale_kernel,
        grid=(n_y,),
        in_specs=[
            pl.BlockSpec((1, aux_local, depth), lambda y: (y, 0, 0)),
            pl.BlockSpec(response.shape, lambda y: (0, 0)),
        ],
        out_specs=pl.BlockSpec((1, 2 * aux_local, depth), lambda y: (y, 0, 0)),
        out_shape=jax.ShapeDtypeStruct((n_y, 2 * aux_local, depth), jnp.bfloat16),
        compiler_params=pltpu.CompilerParams(vmem_limit_bytes=VMEM),
        cost_estimate=SMALL,
    )(coeffs, response)


def product_kernel(core_ref, near_ref, far_ref, scaled_ref, away_ref, kept_ref):
    size = near_ref.shape[0] // 4
    rows = []
    for core in (1 - core_ref[0], core_ref[0]):
        for x in range(2):
            at = pl.multiple_of((2 * x + core) * size, size)
            rows += [ref[pl.ds(at, size)] for ref in (near_ref, far_ref)]
    rows = jnp.concatenate(rows, axis=0)
    half = rows.shape[0] // 2
    for y in range(scaled_ref.shape[0]):
        product = lax.dot_general(
            rows, scaled_ref[y], (((1,), (1,)), ((), ())), preferred_element_type=jnp.float32
        )
        away_ref[y] = product[:half]
        kept_ref[y] = product[half:]


def products(core, near, far, scaled):
    n_rows, depth = near.shape
    n_y, columns, _ = scaled.shape
    rows = pl.BlockSpec((n_rows, depth), lambda y, core: (0, 0))
    return pl.pallas_call(
        product_kernel,
        grid_spec=pltpu.PrefetchScalarGridSpec(
            num_scalar_prefetch=1,
            grid=(n_y // 2,),
            in_specs=[
                rows,
                rows,
                pl.BlockSpec((2, columns, depth), lambda y, core: (y, 0, 0)),
            ],
            out_specs=[pl.BlockSpec((2, n_rows, columns), lambda y, core: (y, 0, 0))] * 2,
        ),
        out_shape=[jax.ShapeDtypeStruct((n_y, n_rows, columns), jnp.float32)] * 2,
        compiler_params=pltpu.CompilerParams(vmem_limit_bytes=VMEM),
        cost_estimate=SMALL,
    )(core, near, far, scaled)


def add_kernel(*refs):
    *refs, out_ref = refs
    for side in range(2):
        total = refs[2 * side][...] + refs[2 * side + 1][...]
        total = total.reshape((out_ref.shape[0], -1, total.shape[-1]))
        out_ref[:, side] = total.astype(out_ref.dtype)


def add_cores(own, partner):
    n_y, n_rows, columns = own[0].shape
    return pl.pallas_call(
        add_kernel,
        grid=(n_y // 2,),
        in_specs=[pl.BlockSpec((2, n_rows, columns), lambda y: (y, 0, 0))] * 4,
        out_specs=pl.BlockSpec((4, 2, n_rows // 2, columns), lambda y: (y, 0, 0, 0)),
        out_shape=jax.ShapeDtypeStruct((2 * n_y, 2, n_rows // 2, columns), SENT),
        compiler_params=pltpu.CompilerParams(vmem_limit_bytes=VMEM),
        cost_estimate=SMALL,
    )(*own, *partner)


def total_kernel(place_ref, parts_ref, out_ref):
    n_y, _, _, _, n_i, n_z, _ = parts_ref.shape
    x_hi, parity = place_ref[0], place_ref[1]
    for i, y, side, odd in itertools.product(range(n_i), range(n_y), range(2), range(2)):
        at = jnp.bitwise_xor(side, x_hi), jnp.bitwise_xor(odd, parity)
        rows = [parts_ref[y, x, at[0], at[1], i].astype(jnp.float32) for x in range(2)]
        rows = rows[0] + rows[1]
        base = (((n_y * i + y) * 2 + side) * 2 * n_z + odd) * 4
        for w in range(2):
            for half in range(2):
                c = (2 * w + half) * LANES
                out_ref[pl.ds(base + 2 * half + w, n_z, stride=8), :] = rows[:, c : c + LANES]


def total_over_x(place, parts):
    n_y, n_x, n_sides, n_parities, n_i, n_z, columns = parts.shape
    n_rows = n_y * n_sides * n_parities * n_z
    out = pl.pallas_call(
        total_kernel,
        grid_spec=pltpu.PrefetchScalarGridSpec(
            num_scalar_prefetch=1,
            grid=(n_i // 2,),
            in_specs=[
                pl.BlockSpec(
                    (n_y, n_x, n_sides, n_parities, 2, n_z, columns),
                    lambda i, place: (0, 0, 0, 0, i, 0, 0),
                )
            ],
            out_specs=pl.BlockSpec((2 * n_rows * 4, LANES), lambda i, place: (i, 0)),
        ),
        out_shape=jax.ShapeDtypeStruct((n_i * n_rows * 4, LANES), jnp.float32),
        compiler_params=pltpu.CompilerParams(vmem_limit_bytes=VMEM),
    )(place, parts)
    out = out.reshape(n_i * n_rows, 2, 2, LANES)
    return jnp.transpose(out, (0, 2, 1, 3)).reshape(-1, 2, 2 * LANES)


def on_device(n_y, n_z, coeffs, occ_index, vir_index, eps_occ, eps_vir, frequencies, offset):
    aux_local, depth = coeffs.shape
    core = lax.axis_index("core").reshape(1).astype(jnp.int32)
    place = jnp.stack([lax.axis_index("x_hi"), lax.axis_index("parity")]).astype(jnp.int32)
    swap = [(0, 1), (1, 0)]

    rows = lax.dynamic_slice_in_dim(coeffs, offset[0], ROWS_DEV, 0)

    coeffs_y = repeat(coeffs, n_y)
    coeffs_y = lax.all_to_all(coeffs_y, "y", 0, 0, tiled=True)

    gathered = lax.all_gather(rows, "half_z", axis=0)
    near = jnp.transpose(gathered, (1, 0, 2)).reshape(-1, depth)
    near_partner = lax.ppermute(near, "x_hi", swap)
    far = lax.ppermute(near, "parity", swap)
    far_partner = lax.ppermute(far, "x_hi", swap)

    energy_gap = lookup(eps_vir, vir_index) - lookup(eps_occ, occ_index)
    squares = frequencies * frequencies
    response = (
        2.0 * energy_gap[None, :] / (energy_gap[None, :] * energy_gap[None, :] + squares[:, None])
    )
    scaled = scale(coeffs_y, response)

    sides = []
    for side in ((near, far), (near_partner, far_partner)):
        away, kept = products(core, *side, scaled)
        sides.append((kept, lax.ppermute(away, "core", swap)))
    parts = lax.all_to_all(add_cores(*sides), ("y", "x_lo"), 0, 0, tiled=True)
    parts = parts.reshape(n_y, 2, 2, 2, ROWS_DEV // 4, n_z // 2, 2 * aux_local)
    return total_over_x(place, parts)


def solution(mesh):
    n_y = 4
    n_z = mesh.shape["aux"] // (2 * n_y)
    split = Mesh(
        mesh.devices.reshape(n_y, 2, n_z // 2, 2, 2, 2),
        ("y", "x_hi", "half_z", "parity", "x_lo", "core"),
    )
    aux, pair = ("y", "x_hi", "half_z", "parity"), ("x_lo", "core")
    return jax.shard_map(
        functools.partial(on_device, n_y, n_z),
        mesh=split,
        in_specs=(P(aux, pair), P(pair), P(pair), P(), P(), P(), P()),
        out_specs=P(pair, None, aux),
        check_vma=False,
    )
```

```python
import functools
import itertools

import jax
import jax.numpy as jnp
from jax import lax
from jax.experimental import pallas as pl
from jax.experimental.pallas import tpu as pltpu
from jax.sharding import Mesh
from jax.sharding import PartitionSpec as P

ROWS_DEV = 16
LANES = 128
SENT = jnp.bfloat16
VMEM = 16 * 1024 * 1024
SMALL = pl.CostEstimate(flops=1, bytes_accessed=1, transcendentals=0)


def lookup(table, index):
    rows = -(-table.shape[0] // LANES)
    rows += -rows % 8
    grid = jnp.pad(table, (0, rows * LANES - table.shape[0])).reshape(rows, LANES)
    high = (index // LANES)[:, None] == jnp.arange(rows, dtype=jnp.int32)[None, :]
    low = (index % LANES)[:, None] == jnp.arange(LANES, dtype=jnp.int32)[None, :]
    picked = lax.dot_general(
        high.astype(jnp.float32),
        grid,
        (((1,), (0,)), ((), ())),
        precision=lax.Precision.HIGHEST,
        preferred_element_type=jnp.float32,
    )
    return jnp.sum(jnp.where(low, picked, 0.0), axis=1)


def repeat_kernel(source_ref, out_ref, block_ref, sems):
    fetch = pltpu.make_async_copy(source_ref, block_ref, sems.at[0])
    fetch.start()
    fetch.wait()
    copies = [
        pltpu.make_async_copy(block_ref, out_ref.at[at], sems.at[at])
        for at in range(out_ref.shape[0])
    ]
    for copy in copies:
        copy.start()
    for copy in copies:
        copy.wait()


def repeat(block, times):
    return pl.pallas_call(
        repeat_kernel,
        in_specs=[pl.BlockSpec(memory_space=pltpu.HBM)],
        out_specs=pl.BlockSpec(memory_space=pltpu.HBM),
        out_shape=jax.ShapeDtypeStruct((times,) + block.shape, block.dtype),
        scratch_shapes=[
            pltpu.VMEM(block.shape, block.dtype),
            pltpu.SemaphoreType.DMA((times,)),
        ],
        compiler_params=pltpu.CompilerParams(vmem_limit_bytes=60 * 1024 * 1024),
        cost_estimate=SMALL,
    )(block)


def scale_kernel(coeffs_ref, response_ref, out_ref):
    coeffs = coeffs_ref[0].astype(jnp.float32)
    aux_local = coeffs.shape[0]
    for w in range(2):
        out_ref[0, w * aux_local : (w + 1) * aux_local] = (
            coeffs * response_ref[w : w + 1, :]
        ).astype(jnp.bfloat16)


def scale(coeffs, response):
    n_y, aux_local, depth = coeffs.shape
    return pl.pallas_call(
        scale_kernel,
        grid=(n_y,),
        in_specs=[
            pl.BlockSpec((1, aux_local, depth), lambda y: (y, 0, 0)),
            pl.BlockSpec(response.shape, lambda y: (0, 0)),
        ],
        out_specs=pl.BlockSpec((1, 2 * aux_local, depth), lambda y: (y, 0, 0)),
        out_shape=jax.ShapeDtypeStruct((n_y, 2 * aux_local, depth), jnp.bfloat16),
        compiler_params=pltpu.CompilerParams(vmem_limit_bytes=VMEM),
        cost_estimate=SMALL,
    )(coeffs, response)


def product_kernel(near_ref, far_ref, scaled_ref, away_ref, kept_ref):
    size = near_ref.shape[0] // 4
    rows = [ref[at * size : (at + 1) * size] for at in range(4) for ref in (near_ref, far_ref)]
    rows = jnp.concatenate(rows, axis=0)
    half = rows.shape[0] // 2
    for y in range(scaled_ref.shape[0]):
        product = lax.dot_general(
            rows, scaled_ref[y], (((1,), (1,)), ((), ())), preferred_element_type=jnp.float32
        )
        away_ref[y] = product[:half]
        kept_ref[y] = product[half:]


def products(near, far, scaled):
    n_rows, depth = near.shape
    n_y, columns, _ = scaled.shape
    rows = pl.BlockSpec((n_rows, depth), lambda y: (0, 0))
    return pl.pallas_call(
        product_kernel,
        grid=(n_y // 2,),
        in_specs=[rows, rows, pl.BlockSpec((2, columns, depth), lambda y: (y, 0, 0))],
        out_specs=[pl.BlockSpec((2, n_rows, columns), lambda y: (y, 0, 0))] * 2,
        out_shape=[jax.ShapeDtypeStruct((n_y, n_rows, columns), jnp.float32)] * 2,
        compiler_params=pltpu.CompilerParams(vmem_limit_bytes=VMEM),
        cost_estimate=SMALL,
    )(near, far, scaled)


def add_kernel(*refs):
    *refs, out_ref = refs
    for side in range(2):
        total = refs[2 * side][...] + refs[2 * side + 1][...]
        total = total.reshape((out_ref.shape[0], -1, total.shape[-1]))
        out_ref[:, side] = total.astype(out_ref.dtype)


def add_cores(own, partner):
    n_y, n_rows, columns = own[0].shape
    return pl.pallas_call(
        add_kernel,
        grid=(n_y // 2,),
        in_specs=[pl.BlockSpec((2, n_rows, columns), lambda y: (y, 0, 0))] * 4,
        out_specs=pl.BlockSpec((4, 2, n_rows // 2, columns), lambda y: (y, 0, 0, 0)),
        out_shape=jax.ShapeDtypeStruct((2 * n_y, 2, n_rows // 2, columns), SENT),
        compiler_params=pltpu.CompilerParams(vmem_limit_bytes=VMEM),
        cost_estimate=SMALL,
    )(*own, *partner)


def total_kernel(place_ref, parts_ref, out_ref):
    n_y, _, _, _, n_i, n_z, _ = parts_ref.shape
    x_hi, parity = place_ref[0], place_ref[1]
    for i, y, side, odd in itertools.product(range(n_i), range(n_y), range(2), range(2)):
        at = jnp.bitwise_xor(side, x_hi), jnp.bitwise_xor(odd, parity)
        rows = [parts_ref[y, x, at[0], at[1], i].astype(jnp.float32) for x in range(2)]
        rows = rows[0] + rows[1]
        base = (((n_y * i + y) * 2 + side) * 2 * n_z + odd) * 4
        for w in range(2):
            for half in range(2):
                c = (2 * w + half) * LANES
                out_ref[pl.ds(base + 2 * half + w, n_z, stride=8), :] = rows[:, c : c + LANES]


def total_over_x(place, parts):
    n_y, n_x, n_sides, n_parities, n_i, n_z, columns = parts.shape
    n_rows = n_y * n_sides * n_parities * n_z
    out = pl.pallas_call(
        total_kernel,
        grid_spec=pltpu.PrefetchScalarGridSpec(
            num_scalar_prefetch=1,
            grid=(n_i // 2,),
            in_specs=[
                pl.BlockSpec(
                    (n_y, n_x, n_sides, n_parities, 2, n_z, columns),
                    lambda i, place: (0, 0, 0, 0, i, 0, 0),
                )
            ],
            out_specs=pl.BlockSpec((2 * n_rows * 4, LANES), lambda i, place: (i, 0)),
        ),
        out_shape=jax.ShapeDtypeStruct((n_i * n_rows * 4, LANES), jnp.float32),
        compiler_params=pltpu.CompilerParams(vmem_limit_bytes=VMEM),
    )(place, parts)
    out = out.reshape(n_i * n_rows, 2, 2, LANES)
    return jnp.transpose(out, (0, 2, 1, 3)).reshape(-1, 2, 2 * LANES)


def on_device(n_y, n_z, coeffs, occ_index, vir_index, eps_occ, eps_vir, frequencies, offset):
    aux_local, depth = coeffs.shape
    core = lax.axis_index("core")
    place = jnp.stack([lax.axis_index("x_hi"), lax.axis_index("parity")]).astype(jnp.int32)
    swap = [(0, 1), (1, 0)]

    rows = lax.dynamic_slice_in_dim(coeffs, offset[0], ROWS_DEV, 0)
    rows = rows.reshape(2, 2, ROWS_DEV // 4, depth)
    first, second = rows[:, 0], rows[:, 1]
    rows = jnp.where(core == 0, jnp.stack([second, first]), jnp.stack([first, second]))
    rows = rows.reshape(ROWS_DEV, depth)

    coeffs_y = repeat(coeffs, n_y)
    coeffs_y = lax.all_to_all(coeffs_y, "y", 0, 0, tiled=True)

    gathered = lax.all_gather(rows, "half_z", axis=0)
    near = jnp.transpose(gathered, (1, 0, 2)).reshape(-1, depth)
    near_partner = lax.ppermute(near, "x_hi", swap)
    far = lax.ppermute(near, "parity", swap)
    far_partner = lax.ppermute(far, "x_hi", swap)

    energy_gap = lookup(eps_vir, vir_index) - lookup(eps_occ, occ_index)
    squares = frequencies * frequencies
    response = (
        2.0 * energy_gap[None, :] / (energy_gap[None, :] * energy_gap[None, :] + squares[:, None])
    )
    scaled = scale(coeffs_y, response)

    sides = []
    for side in ((near, far), (near_partner, far_partner)):
        away, kept = products(*side, scaled)
        sides.append((kept, lax.ppermute(away, "core", swap)))
    parts = lax.all_to_all(add_cores(*sides), ("y", "x_lo"), 0, 0, tiled=True)
    parts = parts.reshape(n_y, 2, 2, 2, ROWS_DEV // 4, n_z // 2, 2 * aux_local)
    return total_over_x(place, parts)


def solution(mesh):
    n_y = 4
    n_z = mesh.shape["aux"] // (2 * n_y)
    split = Mesh(
        mesh.devices.reshape(n_y, 2, n_z // 2, 2, 2, 2),
        ("y", "x_hi", "half_z", "parity", "x_lo", "core"),
    )
    aux, pair = ("y", "x_hi", "half_z", "parity"), ("x_lo", "core")
    return jax.shard_map(
        functools.partial(on_device, n_y, n_z),
        mesh=split,
        in_specs=(P(aux, pair), P(pair), P(pair), P(), P(), P(), P()),
        out_specs=P(pair, None, aux),
        check_vma=False,
    )
```
